128 devices in a mesh: ty: 16 (over x_hi, y, core), tx: 8 (over x_lo, z).
Axes of the slice: x: 4 (x_hi: 2, x_lo: 2; x = x_hi * 2 + x_lo), y: 4, z: 4, core: 2. Of those that a mesh axis runs over, the one named last changes fastest.
Arguments:
- spectrum: float32 [2, 8192, 8192], P(None, 'ty', 'tx'), may hold values from -6 to 6
- pupil: float32 [2, 512, 512], replicated, may hold values from -6 to 6
- amplitudes: float32 [384, 512, 512], P(('ty', 'tx')), may hold values from 0 to 3
- offsets: int32 [384, 2], P(('ty', 'tx')), may hold values from 0 to 7680, as said below
- live: int32 [384], P(('ty', 'tx')), may hold values from 0 to 1, as said below
Outputs:
- spectrum_grad: float32 [2, 8192, 8192], P(None, 'ty', 'tx')
- pupil_grad: float32 [2, 512, 512], replicated
The draws below stay inside these ranges and needn't reach their ends.
Inputs may be any that keep to these rules, and one draw needn't show every extreme that they name: `offsets`: the slots of the device at ty index i and tx index j are i * 8 * 3 + j * 3 to that plus 3 - 1; each such slot's corner has row in [i * 512, (i + 1) * 512) and column in [j * 1024, (j + 1) * 1024), and its window lies inside the spectrum. Each device's live slots come first among its 3 slots, and every device has at least one. Two devices with the same tx index whose ty indices differ by 8 hold together at most 4 live slots; some such pair holds exactly that many, and some device has all 3 slots live.
All inputs are finite; a program needn't handle non-finite values.
Results may differ from the reference program's by a relative error of at most 0.0001.
Values sent between devices are 32-bit elements; how exact they have to be, the bound alone decides.
A program may use at most 192 MiB of HBM per device.

```python
import math
import jax
import jax.numpy as jnp
from jax import lax

M = 512
TR = 512
TC = 1024
CAP = 3
NR = 8192
NC = 8192
SLOTS = 384
N_TY = 16
N_TX = 8


def device_counts(key):
    middle_key = jax.random.fold_in(key, 5)
    row_grid = jnp.broadcast_to(jnp.arange(N_TY)[:, None], (N_TY, N_TX))
    central = (row_grid >= N_TY // 4) & (row_grid < 3 * N_TY // 4)
    edge_count = jnp.ones((N_TY, N_TX), jnp.int32)
    middle = jax.random.randint(middle_key, (N_TY, N_TX), 2, CAP + 1)
    counts = jnp.where(central, middle, edge_count)
    counts = counts.at[N_TY // 2, N_TX // 2].set(CAP)
    return counts.reshape(-1)


def draw_live(key, part):
    counts = device_counts(key)
    slot_ids = jnp.arange(CAP)[None, :]
    return (slot_ids < counts[:, None]).astype(jnp.int32).reshape(-1)


def draw_offsets(key, part):
    key = jax.random.fold_in(key, 7)
    row_key, col_key = jax.random.split(key)
    device_ids = jnp.arange(N_TY * N_TX * CAP) // CAP
    tile_row = device_ids // N_TX
    tile_col = device_ids % N_TX
    row_top = jnp.minimum(TR - 1, TR * N_TY - M - tile_row * TR)
    col_top = jnp.minimum(TC - 1, TC * N_TX - M - tile_col * TC)
    count = N_TY * N_TX * CAP
    row_pick = jax.random.randint(row_key, (count,), 0, row_top + 1)
    col_pick = jax.random.randint(col_key, (count,), 0, col_top + 1)
    last_slot = (N_TY * N_TX - 1) * CAP
    row_pick = row_pick.at[0].set(0).at[last_slot].set(row_top[last_slot])
    col_pick = col_pick.at[0].set(0).at[last_slot].set(col_top[last_slot])
    return jnp.stack([tile_row * TR + row_pick, tile_col * TC + col_pick], axis=1).astype(jnp.int32)


def steps_of(stream_key, dims, cuts, least, largest):
    loudness, own = 1.0, jax.random.fold_in(stream_key, 6)
    for position, blocks in cuts:
        draws = jnp.exp(jax.random.uniform(jax.random.fold_in(own, position), (blocks,), jnp.float32, least / len(cuts), largest / len(cuts)))
        loudness = loudness * jnp.repeat(draws, dims[position] // blocks).reshape([-1 if axis == position else 1 for axis in range(len(dims))])
    return loudness


def noise(key, shape, scale, most, cuts=(), kind=jnp.bfloat16):
    array = jax.random.normal(key, shape, jnp.float32) * scale
    if len(cuts) > 0:
        array = steps_of(key, shape, cuts, -0.22, 0.18) * array
    return jnp.clip(array, min=-most, max=most).astype(kind)


def setup_inputs(seed: int = 0) -> dict:
    streams_of = jax.random.split(jax.random.key(seed), 6)
    return {
        "spectrum": noise(streams_of[0], (2, NR, NC), 1.0, 6.0, ((1, 16), (2, 8)), jnp.float32),
        "pupil": noise(streams_of[1], (2, M, M), 1.0, 6.0, (), jnp.float32),
        "amplitudes": jnp.clip(3.0 * jax.random.uniform(streams_of[2], (SLOTS, M, M), jnp.float32) ** steps_of(streams_of[2], (SLOTS, M, M), ((0, 128),), -0.2, 0.2), 0.0, 3.0),
        "offsets": draw_offsets(jax.random.fold_in(streams_of[5], 71), 0),
        "live": draw_live(jax.random.fold_in(streams_of[5], 71), 0),
    }


def reference(spectrum, pupil, amplitudes, offsets, live):
    pupil_c = lax.complex(pupil[0], pupil[1])
    zero_idx = jnp.zeros((), jnp.int32)

    def one_slot(carried, slot_data):
        spec_grad, pupil_acc = carried
        measured, corner, alive = slot_data
        window = lax.dynamic_slice(spectrum, (zero_idx, corner[0], corner[1]), (2, M, M))
        window_c = lax.complex(window[0], window[1])
        field = jnp.fft.ifft2(window_c * pupil_c, norm='ortho')
        field_re = jnp.real(field)
        field_im = jnp.imag(field)
        modulus = jnp.sqrt(field_re * field_re + field_im * field_im + 1.0)
        residual = (1.0 - measured / modulus) * field
        spectral = jnp.fft.fft2(residual, norm='ortho')
        weight = alive.astype(spectrum.dtype)
        dwin = jnp.conj(pupil_c) * spectral
        dpup = jnp.conj(window_c) * spectral
        dwin_planes = jnp.stack([jnp.real(dwin), jnp.imag(dwin)]) * weight
        dpup_planes = jnp.stack([jnp.real(dpup), jnp.imag(dpup)]) * weight
        current = lax.dynamic_slice(spec_grad, (zero_idx, corner[0], corner[1]), (2, M, M))
        spec_grad = lax.dynamic_update_slice(spec_grad, current + dwin_planes, (zero_idx, corner[0], corner[1]))
        return ((spec_grad, pupil_acc + dpup_planes), None)
    start = (jnp.zeros_like(spectrum), jnp.zeros_like(pupil))
    (spec_grad, pupil_acc), _ = lax.scan(one_slot, start, (amplitudes, offsets, live))
    return (spec_grad, pupil_acc / math.sqrt(N_TY * N_TX))
```

```python
import math
import numpy as np
import ml_dtypes
import jax, jax.numpy as jnp, functools
from jax import lax
from jax.sharding import PartitionSpec as P
from jax.experimental import pallas as pl
from jax.experimental.pallas import tpu as pltpu
F32=jnp.float32; BF=jnp.bfloat16
N_TY = 16
N_TX = 8
M = 512
Q = 128

def tables():
    n=np.arange(Q)[None,:]; k=np.arange(Q)[:,None]
    hi=[];lo=[]
    for q in range(4):
        ang=2*np.pi*((n*(4*k+q))%M)/M
        c=np.cos(ang)/math.sqrt(M); s=np.sin(ang)/math.sqrt(M)
        m=np.block([[c,-s],[s,c]])
        h=m.astype(ml_dtypes.bfloat16); l=(m-h.astype(np.float64)).astype(ml_dtypes.bfloat16)
        hi.append(h); lo.append(l)
    hi=np.stack(hi); lo=np.stack(lo)
    perm=np.zeros((M,M),ml_dtypes.bfloat16)
    for q in range(4):
        for j in range(Q): perm[4*j+q,q*Q+j]=1
    T=lambda a: np.ascontiguousarray(np.swapaxes(a,1,2))
    return hi,lo,T(hi),T(lo),perm

def split(x):
    h=x.astype(BF)
    return h,(x-h.astype(F32)).astype(BF)

def dot(a,b):
    return jnp.dot(a,b,preferred_element_type=F32)

def lmul(mh,ml,y):
    h,l=split(y)
    return dot(jnp.concatenate([mh,ml,mh],axis=1),jnp.concatenate([h,h,l],axis=0))

def rmul(y,mh,ml):
    h,l=split(y)
    return dot(jnp.concatenate([h,l,h],axis=1),jnp.concatenate([mh,mh,ml],axis=0))

def fly_in(xr,xi):
    a=(xr[0]+xr[2],xi[0]+xi[2]); b=(xr[0]-xr[2],xi[0]-xi[2])
    c=(xr[1]+xr[3],xi[1]+xi[3]); d=(xr[1]-xr[3],xi[1]-xi[3])
    return [(a[0]+c[0],a[1]+c[1]),(b[0]-d[1],b[1]+d[0]),(a[0]-c[0],a[1]-c[1]),(b[0]+d[1],b[1]-d[0])]

def fly_out(e):
    a=(e[0][0]+e[2][0],e[0][1]+e[2][1]); b=(e[0][0]-e[2][0],e[0][1]-e[2][1])
    c=(e[1][0]+e[3][0],e[1][1]+e[3][1]); d=(e[1][0]-e[3][0],e[1][1]-e[3][1])
    return [(a[0]+c[0],a[1]+c[1]),(b[0]+d[1],b[1]-d[0]),(a[0]-c[0],a[1]-c[1]),(b[0]-d[1],b[1]+d[0])]

CB=256; RB=256

def rows_from(ref,p,start):
    low=lax.rem(start,8)
    x=ref[p,pl.ds(pl.multiple_of(start-low,8),Q+8),:]
    return pltpu.roll(x,lax.rem(Q+8-low,Q+8),0)[:Q]

def kern2(off, live, X_h, R_h, L_h, C_h, amp_h, pup_h, mh, ml, th, tl, pm, pt, G_h, DP_h,
          X, G, A, AP, PP, PR, W, H, D, DP, sem, osem):
    cps=[]
    for i,(s,d) in enumerate([(pup_h,PP.at[:,0:M]),(pup_h,PP.at[:,M:2*M]),(amp_h,A),
                 (X_h,X.at[:,0:M,0:1024]),(R_h,X.at[:,0:M,1024:1536]),
                 (L_h,X.at[:,M:2*M,0:1024]),(C_h,X.at[:,M:2*M,1024:1536])]):
        cp=pltpu.make_async_copy(s,d,sem.at[i]); cp.start(); cps.append(cp)
    r0=lax.axis_index("ty")*512; c0_=lax.axis_index("tx")*1024
    @pl.loop(0,16)
    def _(i):
        G[:,pl.ds(pl.multiple_of(i*64,64),64),:]=jnp.zeros((2,64,1536),F32)
    DP[...]=jnp.zeros((2,M,M),F32)
    for cp in cps[0:3]: cp.wait()
    @pl.loop(0,3)
    def _(s):
        @pl.when(live[s]>0)
        def _():
            for q in range(2):
                h,l=split(A[s,q*RB:(q+1)*RB,:])
                H[0,q*RB:(q+1)*RB,:]=dot(jnp.concatenate([h,l],axis=1),jnp.concatenate([pm[...],pm[...]],axis=0))
            for q in range(2):
                h,l=split(H[0,:,q*RB:(q+1)*RB])
                AP[s,:,q*RB:(q+1)*RB]=dot(jnp.concatenate([pt[...],pt[...]],axis=1),jnp.concatenate([h,l],axis=0))
    for cp in cps[3:]: cp.wait()
    @pl.loop(0,3)
    def _(s):
        @pl.when(live[s]>0)
        def _():
            r=off[s,0]-r0; c=off[s,1]-c0_
            qc=c//M; c0=c-qc*M
            @pl.loop(0,4)
            def _(b):
                for p in range(2):
                    x=rows_from(PP,p,lax.rem(M-r,M)+b*Q)
                    PR[p,pl.ds(pl.multiple_of(b*Q,Q),Q),:]=pltpu.roll(x,c0,1)
            @pl.loop(0,M//CB)
            def _(j):
                cols=pl.ds(pl.multiple_of(j*CB,CB),CB)
                b1=pl.ds(pl.multiple_of(qc*M+j*CB,CB),CB); b2=pl.ds(pl.multiple_of(qc*M+M+j*CB,CB),CB)
                mc=lax.broadcasted_iota(jnp.int32,(Q,CB),1)+j*CB>=c0
                xr=[];xi=[]
                for m in range(4):
                    mr=lax.broadcasted_iota(jnp.int32,(Q,CB),0)+m*Q>=r
                    w=[]
                    for p in range(2):
                        rt=slice(m*Q,(m+1)*Q); rl=slice(M+m*Q,M+(m+1)*Q)
                        v=jnp.where(mr,jnp.where(mc,X[p,rt,b1],X[p,rt,b2]),jnp.where(mc,X[p,rl,b1],X[p,rl,b2]))
                        W[p,rt,cols]=v; w.append(v)
                    pr=PR[0,rt,cols]; pi=PR[1,rt,cols]
                    xr.append(w[0]*pr-w[1]*pi); xi.append(w[0]*pi+w[1]*pr)
                for q,(yr,yi) in enumerate(fly_in(xr,xi)):
                    o=lmul(mh[q],ml[q],jnp.concatenate([yr,yi],axis=0))
                    H[0,q*Q:(q+1)*Q,cols]=o[:Q]; H[1,q*Q:(q+1)*Q,cols]=o[Q:]
            @pl.loop(0,M//RB)
            def _(j):
                rows=pl.ds(pl.multiple_of(j*RB,RB),RB)
                xr=[H[0,rows,m*Q:(m+1)*Q] for m in range(4)]; xi=[H[1,rows,m*Q:(m+1)*Q] for m in range(4)]
                e=[]
                for q,(yr,yi) in enumerate(fly_in(xr,xi)):
                    f=rmul(jnp.concatenate([yr,yi],axis=1),th[q],tl[q])
                    fr=f[:,:Q]; fi=f[:,Q:]
                    fac=1.0-AP[s,rows,q*Q:(q+1)*Q]*lax.rsqrt(fr*fr+fi*fi+1.0)
                    o=rmul(jnp.concatenate([fac*fr,fac*fi],axis=1),mh[q],ml[q])
                    e.append((o[:,:Q],o[:,Q:]))
                for m,(zr,zi) in enumerate(fly_out(e)):
                    H[0,rows,m*Q:(m+1)*Q]=zr; H[1,rows,m*Q:(m+1)*Q]=zi
            @pl.loop(0,M//CB)
            def _(j):
                cols=pl.ds(pl.multiple_of(j*CB,CB),CB)
                b1=pl.ds(pl.multiple_of(qc*M+j*CB,CB),CB); b2=pl.ds(pl.multiple_of(qc*M+M+j*CB,CB),CB)
                mc=lax.broadcasted_iota(jnp.int32,(Q,CB),1)+j*CB>=c0
                e=[]
                for q in range(4):
                    o=lmul(th[q],tl[q],jnp.concatenate([H[0,q*Q:(q+1)*Q,cols],H[1,q*Q:(q+1)*Q,cols]],axis=0))
                    e.append((o[:Q],o[Q:]))
                for m,(sr,si) in enumerate(fly_out(e)):
                    mr=lax.broadcasted_iota(jnp.int32,(Q,CB),0)+m*Q>=r
                    rt=slice(m*Q,(m+1)*Q); rl=slice(M+m*Q,M+(m+1)*Q)
                    pr=PR[0,rt,cols]; pi=PR[1,rt,cols]
                    wr=W[0,rt,cols]; wi=W[1,rt,cols]
                    g=(pr*sr+pi*si,pr*si-pi*sr); d=(wr*sr+wi*si,wr*si-wi*sr)
                    for p in range(2):
                        D[p,rt,cols]=d[p]; D[p,rl,cols]=d[p]
                        gt=jnp.where(mr,g[p],0.0); gl=g[p]-gt
                        g1=jnp.where(mc,gt,0.0); G[p,rt,b1]+=g1; G[p,rt,b2]+=gt-g1
                        g1=jnp.where(mc,gl,0.0); G[p,rl,b1]+=g1; G[p,rl,b2]+=gl-g1
            @pl.loop(0,4)
            def _(b):
                for p in range(2):
                    x=rows_from(D,p,r+b*Q)
                    DP[p,pl.ds(pl.multiple_of(b*Q,Q),Q),:]+=pltpu.roll(x,lax.rem(M-c0,M),1)
    o1=pltpu.make_async_copy(G,G_h,osem.at[0]); o2=pltpu.make_async_copy(DP,DP_h,osem.at[1])
    o1.start(); o2.start(); o1.wait(); o2.wait()

def compute(off,live,X,R,L,C,amp,pup):
    hi,lo,th,tl,pm=[jnp.asarray(t) for t in tables()]
    sm=pl.BlockSpec(memory_space=pltpu.SMEM); an=pl.BlockSpec(memory_space=pl.ANY); vm=pl.BlockSpec(memory_space=pltpu.VMEM)
    V=pltpu.VMEM
    return pl.pallas_call(kern2,
        out_shape=[jax.ShapeDtypeStruct((2,1024,1536),F32),jax.ShapeDtypeStruct((2,M,M),F32)],
        in_specs=[sm,sm]+[an]*6+[vm]*6, out_specs=[an,an],
        scratch_shapes=[V((2,1024,1536),F32),V((2,1024,1536),F32),V((3,M,M),F32),V((3,M,M),F32),V((2,2*M,M),F32),
            V((2,M,M),F32),V((2,M,M),F32),V((2,M,M),F32),V((2,2*M,M),F32),V((2,M,M),F32),
            pltpu.SemaphoreType.DMA((7,)),pltpu.SemaphoreType.DMA((2,))],
        compiler_params=pltpu.CompilerParams(vmem_limit_bytes=62*1024*1024),
        name="slots",
        cost_estimate=pl.CostEstimate(flops=3*4*3*2*512*512*256,bytes_accessed=31*2**20,transcendentals=3*512*512))(off,live,X,R,L,C,amp,pup,hi,lo,th,tl,pm,pm.T)


MESH = pl.DeviceIdType.MESH
LOW = pl.ds(0, 256)
HIGH = pl.ds(256, 256)
LEFT = pl.ds(0, 512)
RIGHT = pl.ds(512, 512)
WHOLE = pl.ds(0, 512)


def when(cond, run):
    pl.when(cond)(run)


def greet(partners):
    barrier = pltpu.get_barrier_semaphore()
    count = jnp.int32(0)
    for cond, device in partners:
        count = count + jnp.where(cond, 1, 0).astype(jnp.int32)

        @pl.when(cond)
        def _():
            pl.semaphore_signal(barrier, inc=1, device_id=device, device_id_type=MESH)

    pl.semaphore_wait(barrier, count)


class Place:
    def __init__(self):
        ty = lax.axis_index("ty")
        tx = lax.axis_index("tx")
        self.ty, self.tx = ty, tx
        self.has_u, self.has_d = ty > 0, ty < N_TY - 1
        self.has_l, self.has_r = tx > 0, tx < N_TX - 1
        self.odd = lax.rem(ty, 2) == 1
        self.even = lax.rem(ty, 2) == 0
        self.up, self.down = (ty - 1, tx), (ty + 1, tx)
        self.left, self.right = (ty, tx - 1), (ty, tx + 1)

    def neighbours(self):
        return [
            (self.has_u, self.up),
            (self.has_d, self.down),
            (self.has_l, self.left),
            (self.has_r, self.right),
        ]


def fetch_kernel(tile, strip_r, strip_l, strip_c, relay_l, relay_r, ss, rs):
    me = Place()
    ty, tx = me.ty, me.tx
    yh, xh = N_TY // 2, N_TX // 2
    y_from, y_via, y_to = ty == yh, ty == N_TY - 1, ty == yh - 1
    x_from, x_via, x_to = tx == xh, tx == N_TX - 1, tx == xh - 1
    greet(
        me.neighbours()
        + [
            (y_from, (N_TY - 1, tx)),
            (y_via, (yh, tx)),
            (y_via, (yh - 1, tx)),
            (y_to, (N_TY - 1, tx)),
            (x_from, (ty, N_TX - 1)),
            (x_via, (ty, xh)),
            (x_via, (ty, xh - 1)),
            (x_to, (ty, N_TX - 1)),
        ]
    )

    def rc(k, src, dst, dev, rk=None):
        return pltpu.make_async_remote_copy(
            src_ref=src,
            dst_ref=dst,
            send_sem=ss.at[k],
            recv_sem=rs.at[k if rk is None else rk],
            device_id=dev,
            device_id_type=MESH,
        )

    ra = rc(0, tile.at[:, LOW, LEFT], strip_r.at[:, LOW, :], me.left)
    rb = rc(1, tile.at[:, HIGH, LEFT], strip_r.at[:, HIGH, :], me.left)
    rb_out = rc(1, tile.at[:, HIGH, LEFT], relay_r, (ty, N_TX - 1), 10)
    rb_fwd = rc(10, relay_r, strip_r.at[:, HIGH, :], (ty, xh - 1), 1)
    l0b = rc(2, tile.at[:, HIGH, LEFT], strip_l.at[:, HIGH, LEFT], me.up)
    l0a = rc(3, tile.at[:, LOW, LEFT], strip_l.at[:, LOW, LEFT], me.up)
    l1 = [
        rc(4, tile.at[:, LOW, RIGHT], strip_l.at[:, LOW, RIGHT], me.up),
        rc(5, tile.at[:, HIGH, RIGHT], strip_l.at[:, HIGH, RIGHT], me.up),
    ]
    l1_out = [
        rc(4, tile.at[:, LOW, RIGHT], relay_l.at[:, LOW, :], (N_TY - 1, tx), 8),
        rc(5, tile.at[:, HIGH, RIGHT], relay_l.at[:, HIGH, :], (N_TY - 1, tx), 9),
    ]
    l1_fwd = [
        rc(8, relay_l.at[:, LOW, :], strip_l.at[:, LOW, RIGHT], (yh - 1, tx), 4),
        rc(9, relay_l.at[:, HIGH, :], strip_l.at[:, HIGH, RIGHT], (yh - 1, tx), 5),
    ]
    ca = rc(6, strip_r.at[:, LOW, :], strip_c.at[:, LOW, :], me.up)
    cb = rc(7, strip_r.at[:, HIGH, :], strip_c.at[:, HIGH, :], me.up)
    cz = rc(7, strip_l.at[:, HIGH, LEFT], strip_c.at[:, HIGH, :], me.left)

    when(me.has_l, ra.start)
    when(me.has_u, l0b.start)
    when(me.has_l & (tx != xh), rb.start)
    when(x_from, rb_out.start)
    for direct, out in zip(l1, l1_out):
        when(me.has_u & (ty != yh), direct.start)
        when(y_from, out.start)
    when(me.has_u, l0a.start)

    when(me.has_r, ra.wait_recv)
    when(me.has_r & me.has_u, ca.start)
    when(me.has_d, l0b.wait_recv)
    when(me.has_d & me.has_l & me.odd, cz.start)

    def pass_rb():
        rb_out.wait_recv()
        rb_fwd.start()

    when(x_via, pass_rb)
    for out, fwd in zip(l1_out, l1_fwd):

        def pass_l1():
            out.wait_recv()
            fwd.start()

        when(y_via, pass_l1)
    when(me.has_r, rb.wait_recv)
    when(me.has_r & me.has_u & me.odd, cb.start)

    def rest():
        l0a.wait_recv()
        l1[0].wait_recv()
        l1[1].wait_recv()

    when(me.has_d, rest)
    when(me.has_d & me.has_r, ca.wait_recv)
    when(me.has_d & me.has_r, cz.wait_recv)
    when(me.has_l, ra.wait_send)
    when(me.has_l, rb.wait_send)

    def sent_l():
        l0b.wait_send()
        l0a.wait_send()
        l1[0].wait_send()
        l1[1].wait_send()

    when(me.has_u, sent_l)
    when(me.has_r & me.has_u, ca.wait_send)
    when(me.has_r & me.has_u & me.odd, cb.wait_send)
    when(me.has_d & me.has_l & me.odd, cz.wait_send)
    when(x_via, rb_fwd.wait_send)

    def sent_fwd():
        l1_fwd[0].wait_send()
        l1_fwd[1].wait_send()

    when(y_via, sent_fwd)


def fetch(tile):
    return pl.pallas_call(
        fetch_kernel,
        out_shape=[
            jax.ShapeDtypeStruct((2, M, M), F32),
            jax.ShapeDtypeStruct((2, M, 2 * M), F32),
            jax.ShapeDtypeStruct((2, M, M), F32),
        ],
        in_specs=[pl.BlockSpec(memory_space=pl.ANY)],
        out_specs=[pl.BlockSpec(memory_space=pl.ANY)] * 3,
        scratch_shapes=[
            pltpu.VMEM((2, M, M), F32),
            pltpu.VMEM((2, M // 2, M), F32),
            pltpu.SemaphoreType.DMA((11,)),
            pltpu.SemaphoreType.DMA((11,)),
        ],
        name="fetch_strips",
        compiler_params=pltpu.CompilerParams(collective_id=0, has_side_effects=True),
    )(tile)


def give_kernel(
    grads, dpup, out, pup, own, g_r, g_l, got_l, got_r, got_c, got_z, relay_l, relay_r, part, sums, rows_a, rows_b, rows_c, ls, ss, rs, ps, pr
):
    me = Place()
    ty, tx = me.ty, me.tx
    yh, xh = N_TY // 2, N_TX // 2
    y_from, y_via, y_to = ty == yh - 1, ty == 0, ty == yh
    x_from, x_via, x_to = tx == xh - 1, tx == 0, tx == xh
    core = lax.rem(ty, 2)
    x = (ty // 8) * 2 + tx // 4
    y = lax.rem(ty, 8) // 2
    z = lax.rem(tx, 4)

    def device(px, py, pz):
        return ((px // 2) * 8 + py * 2 + core, lax.rem(px, 2) * 4 + pz)

    mate = (ty + 1 - 2 * core, tx)
    peers_x = [device(lax.rem(x + d, 4), y, z) for d in (1, 2, 3)]
    peers_y = [device(x, lax.rem(y + d, 4), z) for d in (1, 2, 3)]
    peers_z = [device(x, y, lax.rem(z + d, 4)) for d in (1, 2, 3)]
    always = ty >= 0
    greet(
        me.neighbours()
        + [
            (y_from, (0, tx)),
            (y_via, (yh - 1, tx)),
            (y_via, (yh, tx)),
            (y_to, (0, tx)),
            (x_from, (ty, 0)),
            (x_via, (ty, xh - 1)),
            (x_via, (ty, xh)),
            (x_to, (ty, 0)),
        ]
        + [(always, d) for d in [mate] + peers_x + peers_y + peers_z]
    )

    def rc(k, src, dst, dev, rk=None):
        return pltpu.make_async_remote_copy(
            src_ref=src,
            dst_ref=dst,
            send_sem=ss.at[k],
            recv_sem=rs.at[k if rk is None else rk],
            device_id=dev,
            device_id_type=MESH,
        )

    def pc(k, src, dst, dev):
        return pltpu.make_async_remote_copy(
            src_ref=src,
            dst_ref=dst,
            send_sem=ps.at[k],
            recv_sem=pr.at[k],
            device_id=dev,
            device_id_type=MESH,
        )

    top = pl.ds(M, 256)
    bottom = pl.ds(M + 256, 256)
    far = pl.ds(2 * M, M)
    load_p = pltpu.make_async_copy(dpup.at[core], part, ls.at[0])
    load_r = pltpu.make_async_copy(grads.at[:, WHOLE, far], g_r, ls.at[1])
    load_l = pltpu.make_async_copy(grads.at[:, bottom, LEFT], g_l, ls.at[2])
    load_o = pltpu.make_async_copy(grads.at[:, WHOLE, pl.ds(0, 2 * M)], own, ls.at[3])

    pair = pc(0, dpup.at[1 - core], sums, mate)
    ca = rc(0, grads.at[:, top, far], got_c.at[:, LOW, :], me.down)
    cb = rc(1, grads.at[:, bottom, far], got_c.at[:, HIGH, :], me.down)
    cz = rc(1, grads.at[:, bottom, far], got_z, me.right, 2)
    l0a = rc(3, grads.at[:, top, LEFT], got_l.at[:, LOW, LEFT], me.down)
    l0b = rc(4, g_l, got_l.at[:, HIGH, LEFT], me.down)
    l1 = [
        rc(5, grads.at[:, top, RIGHT], got_l.at[:, LOW, RIGHT], me.down),
        rc(6, grads.at[:, bottom, RIGHT], got_l.at[:, HIGH, RIGHT], me.down),
    ]
    l1_out = [
        rc(5, grads.at[:, top, RIGHT], relay_l.at[:, LOW, :], (0, tx), 9),
        rc(6, grads.at[:, bottom, RIGHT], relay_l.at[:, HIGH, :], (0, tx), 10),
    ]
    l1_fwd = [
        rc(9, relay_l.at[:, LOW, :], got_l.at[:, LOW, RIGHT], (yh, tx), 5),
        rc(10, relay_l.at[:, HIGH, :], got_l.at[:, HIGH, RIGHT], (yh, tx), 6),
    ]
    ra = rc(7, g_r.at[:, LOW, :], got_r.at[:, LOW, :], me.right)
    rb = rc(8, g_r.at[:, HIGH, :], got_r.at[:, HIGH, :], me.right)
    ra_out = rc(7, g_r.at[:, LOW, :], relay_r, (ty, 0), 11)
    ra_fwd = rc(11, relay_r, got_r.at[:, LOW, :], (ty, xh), 7)

    load_p.start()
    load_r.start()
    load_l.start()
    pair.start()
    has_c = me.has_d & me.has_r
    when(has_c, ca.start)
    when(has_c & me.even, cb.start)
    when(has_c & me.odd, cz.start)
    for direct, out_l in zip(l1, l1_out):
        when(me.has_d & (ty != yh - 1), direct.start)
        when(y_from, out_l.start)
    when(me.has_d, l0a.start)
    load_o.start()

    load_r.wait()
    load_l.wait()
    when(me.has_r & me.even, rb.start)
    when(me.has_d & (me.even | (tx == 0)), l0b.start)

    load_p.wait()
    pair.wait_recv()
    sums[...] += part[...]

    quarter = M // 4

    def share(base, step, peers, src, dst, rows, mine):
        copies = []
        for d in range(3):
            to = lax.rem(mine + d + 1, 4)
            copies.append(
                pc(base + d, src.at[pl.ds(pl.multiple_of(to * rows, rows), rows), :], dst.at[d], peers[d])
            )
        for copy in copies:
            copy.start()
        return copies

    def own_rows(src, rows, mine):
        return src[pl.ds(pl.multiple_of(mine * rows, rows), rows), :]

    sent = share(1, 0, peers_x, sums, rows_a, 128, x)

    def add_c_low():
        ca.wait_recv()
        g_r[:, LOW, :] += got_c[:, LOW, :]

    when(me.has_u & me.has_r, add_c_low)
    when(me.has_r & (tx != xh - 1), ra.start)
    when(x_from, ra_out.start)

    def add_c_high():
        cb.wait_recv()
        g_r[:, HIGH, :] += got_c[:, HIGH, :]
        rb.start()

    when(me.has_r & me.odd, add_c_high)

    def add_z():
        cz.wait_recv()
        g_l[...] += got_z[...]
        l0b.start()

    when(me.has_d & me.odd & (tx > 0), add_z)

    for copy in sent:
        copy.wait_recv()
    part[0:128, :] = own_rows(sums, 128, x) + rows_a[0] + rows_a[1] + rows_a[2]
    sent_y = share(4, 1, peers_y, part, rows_b, 32, y)

    def pass_ra():
        ra_out.wait_recv()
        ra_fwd.start()

    when(x_via, pass_ra)
    for out_l, fwd in zip(l1_out, l1_fwd):

        def pass_l1():
            out_l.wait_recv()
            fwd.start()

        when(y_via, pass_l1)

    for copy in sent_y:
        copy.wait_recv()
    part[128:160, :] = own_rows(part, 32, y) + rows_b[0] + rows_b[1] + rows_b[2]
    sent_z = share(7, 2, peers_z, part.at[pl.ds(128, 32)], rows_c, 8, z)
    for copy in sent_z:
        copy.wait_recv()
    norm = 1.0 / math.sqrt(N_TY * N_TX)
    base = x * 128 + y * 32 + z * 8
    total = own_rows(part.at[pl.ds(128, 32)], 8, z) + rows_c[0] + rows_c[1] + rows_c[2]
    pup[core, pl.ds(pl.multiple_of(base, 8), 8), :] = total * norm

    def spread(base_k, start, rows, peers):
        here = pup.at[core, pl.ds(pl.multiple_of(start, rows), rows), :]
        copies = [pc(base_k + d, here, here, peers[d]) for d in range(3)]
        for copy in copies:
            copy.start()
        for copy in copies:
            copy.wait_recv()
        return copies

    all_sent = sent + sent_y + sent_z
    all_sent += spread(10, base, 8, peers_z)
    all_sent += spread(13, x * 128 + y * 32, 32, peers_y)
    all_sent += spread(16, x * 128, 128, peers_x)
    last = pc(19, pup.at[core], pup.at[core], mate)
    last.start()

    load_o.wait()

    def add_l():
        l0a.wait_recv()
        l0b.wait_recv()
        l1[0].wait_recv()
        l1[1].wait_recv()

    when(me.has_u, add_l)

    def add_r():
        ra.wait_recv()
        rb.wait_recv()

    when(me.has_l, add_r)

    @pl.loop(0, 16)
    def _(i):
        rows = pl.ds(pl.multiple_of(i * 32, 32), 32)
        out[:, rows, :] = own[:, rows, :]

        @pl.when(me.has_u)
        def _():
            out[:, rows, :] += got_l[:, rows, :]

        @pl.when(me.has_l)
        def _():
            out[:, rows, 0:M] += got_r[:, rows, :]

    last.wait_recv()
    pair.wait_send()
    last.wait_send()
    for copy in all_sent:
        copy.wait_send()
    when(has_c, ca.wait_send)
    when(has_c, cb.wait_send)

    def sent_l():
        l0a.wait_send()
        l0b.wait_send()
        l1[0].wait_send()
        l1[1].wait_send()

    when(me.has_d, sent_l)

    def sent_r():
        ra.wait_send()
        rb.wait_send()

    when(me.has_r, sent_r)
    when(x_via, ra_fwd.wait_send)

    def sent_fwd():
        l1_fwd[0].wait_send()
        l1_fwd[1].wait_send()

    when(y_via, sent_fwd)


def give(grads, dpup):
    vmem = pltpu.VMEM
    return pl.pallas_call(
        give_kernel,
        out_shape=[
            jax.ShapeDtypeStruct((2, M, 2 * M), F32),
            jax.ShapeDtypeStruct((2, M, M), F32),
        ],
        in_specs=[pl.BlockSpec(memory_space=pl.ANY)] * 2,
        out_specs=[pl.BlockSpec(memory_space=pltpu.VMEM)] * 2,
        scratch_shapes=[
            vmem((2, M, 2 * M), F32),
            vmem((2, M, M), F32),
            vmem((2, M // 2, M), F32),
            vmem((2, M, 2 * M), F32),
            vmem((2, M, M), F32),
            vmem((2, M, M), F32),
            vmem((2, M // 2, M), F32),
            vmem((2, M, M), F32),
            vmem((2, M // 2, M), F32),
            vmem((M, M), F32),
            vmem((M, M), F32),
            vmem((3, 128, M), F32),
            vmem((3, 32, M), F32),
            vmem((3, 8, M), F32),
            pltpu.SemaphoreType.DMA((4,)),
            pltpu.SemaphoreType.DMA((12,)),
            pltpu.SemaphoreType.DMA((12,)),
            pltpu.SemaphoreType.DMA((20,)),
            pltpu.SemaphoreType.DMA((20,)),
        ],
        name="give_back",
        compiler_params=pltpu.CompilerParams(
            collective_id=1, has_side_effects=True, vmem_limit_bytes=60 * 1024 * 1024
        ),
    )(grads, dpup)


def body(spectrum, pupil, amplitudes, offsets, live):
    strip_r, strip_l, strip_c = fetch(spectrum)
    grads, dpup = compute(offsets, live, spectrum, strip_r, strip_l, strip_c, amplitudes, pupil)
    return tuple(give(grads, dpup))


def solution(mesh):
    return jax.shard_map(
        body,
        mesh=mesh,
        in_specs=(
            P(None, "ty", "tx"),
            P(),
            P(("ty", "tx"), None, None),
            P(("ty", "tx"), None),
            P(("ty", "tx")),
        ),
        out_specs=(P(None, "ty", "tx"), P()),
        check_vma=False,
    )
```

```python
import math
import numpy as np
import ml_dtypes
import jax, jax.numpy as jnp, functools
from jax import lax
from jax.sharding import PartitionSpec as P
from jax.experimental import pallas as pl
from jax.experimental.pallas import tpu as pltpu
F32=jnp.float32; BF=jnp.bfloat16
N_TY = 16
N_TX = 8
M = 512
Q = 128

def tables():
    n=np.arange(Q)[None,:]; k=np.arange(Q)[:,None]
    hi=[];lo=[]
    for q in range(4):
        ang=2*np.pi*((n*(4*k+q))%M)/M
        c=np.cos(ang)/math.sqrt(M); s=np.sin(ang)/math.sqrt(M)
        m=np.block([[c,-s],[s,c]])
        h=m.astype(ml_dtypes.bfloat16); l=(m-h.astype(np.float64)).astype(ml_dtypes.bfloat16)
        hi.append(h); lo.append(l)
    hi=np.stack(hi); lo=np.stack(lo)
    perm=np.zeros((M,M),ml_dtypes.bfloat16)
    for q in range(4):
        for j in range(Q): perm[4*j+q,q*Q+j]=1
    T=lambda a: np.ascontiguousarray(np.swapaxes(a,1,2))
    return hi,lo,T(hi),T(lo),perm

def split(x):
    h=x.astype(BF)
    return h,(x-h.astype(F32)).astype(BF)

def dot(a,b):
    return jnp.dot(a,b,preferred_element_type=F32)

def lmul(mh,ml,y):
    h,l=split(y)
    return dot(jnp.concatenate([mh,ml,mh],axis=1),jnp.concatenate([h,h,l],axis=0))

def rmul(y,mh,ml):
    h,l=split(y)
    return dot(jnp.concatenate([h,l,h],axis=1),jnp.concatenate([mh,mh,ml],axis=0))

def fly_in(xr,xi):
    a=(xr[0]+xr[2],xi[0]+xi[2]); b=(xr[0]-xr[2],xi[0]-xi[2])
    c=(xr[1]+xr[3],xi[1]+xi[3]); d=(xr[1]-xr[3],xi[1]-xi[3])
    return [(a[0]+c[0],a[1]+c[1]),(b[0]-d[1],b[1]+d[0]),(a[0]-c[0],a[1]-c[1]),(b[0]+d[1],b[1]-d[0])]

def fly_out(e):
    a=(e[0][0]+e[2][0],e[0][1]+e[2][1]); b=(e[0][0]-e[2][0],e[0][1]-e[2][1])
    c=(e[1][0]+e[3][0],e[1][1]+e[3][1]); d=(e[1][0]-e[3][0],e[1][1]-e[3][1])
    return [(a[0]+c[0],a[1]+c[1]),(b[0]+d[1],b[1]-d[0]),(a[0]-c[0],a[1]-c[1]),(b[0]-d[1],b[1]+d[0])]


def permute(load, mid, store, left, right):
    for q in range(2):
        part = slice(q * 256, (q + 1) * 256)
        h, l = split(load(part))
        mid[part, :] = dot(jnp.concatenate([h, l], axis=1), jnp.concatenate([right, right], axis=0))
    for q in range(2):
        part = slice(q * 256, (q + 1) * 256)
        h, l = split(mid[:, part])
        store(part, dot(jnp.concatenate([left, left], axis=1), jnp.concatenate([h, l], axis=0)))


def shifted(by, axis):
    a = lax.broadcasted_iota(jnp.int32, (M, M), axis)
    b = lax.broadcasted_iota(jnp.int32, (M, M), 1 - axis) + by
    b = jnp.where(b >= M, b - M, b)
    return jnp.where(a == b, 1.0, 0.0).astype(BF)


MESH = pl.DeviceIdType.MESH
LOW = pl.ds(0, 256)
HIGH = pl.ds(256, 256)
LEFT = pl.ds(0, 512)
RIGHT = pl.ds(512, 512)
WHOLE = pl.ds(0, 512)


def when(cond, run):
    pl.when(cond)(run)


def greet(partners):
    barrier = pltpu.get_barrier_semaphore()
    count = jnp.int32(0)
    for cond, device in partners:
        count = count + jnp.where(cond, 1, 0).astype(jnp.int32)

        @pl.when(cond)
        def _():
            pl.semaphore_signal(barrier, inc=1, device_id=device, device_id_type=MESH)

    pl.semaphore_wait(barrier, count)


class Place:
    def __init__(self):
        ty = lax.axis_index("ty")
        tx = lax.axis_index("tx")
        self.ty, self.tx = ty, tx
        self.has_u, self.has_d = ty > 0, ty < N_TY - 1
        self.has_l, self.has_r = tx > 0, tx < N_TX - 1
        self.odd = lax.rem(ty, 2) == 1
        self.even = lax.rem(ty, 2) == 0
        self.up, self.down = (ty - 1, tx), (ty + 1, tx)
        self.left, self.right = (ty, tx - 1), (ty, tx + 1)

    def neighbours(self):
        return [
            (self.has_u, self.up),
            (self.has_d, self.down),
            (self.has_l, self.left),
            (self.has_r, self.right),
        ]


def slots_kernel(
    off, live, tile, amp, pup, mh, ml, th, tl, pm, pt, grads, dpup,
    X, G, A, AP, PP, PR, W, H, D, DP, relay_l, relay_a, relay_r, ls, ss, rs
):
    strip_r = X.at[:, 0:M, 2 * M : 3 * M]
    strip_l = X.at[:, M : 2 * M, 0 : 2 * M]
    strip_c = X.at[:, M : 2 * M, 2 * M : 3 * M]
    me = Place()
    ty, tx = me.ty, me.tx
    yh, xh = N_TY // 2, N_TX // 2
    y_from, y_via, y_to = ty == yh, ty == N_TY - 1, ty == yh - 1
    x_from, x_via, x_to = tx == xh, tx == N_TX - 1, tx == xh - 1
    greet(
        me.neighbours()
        + [
            (y_from, (N_TY - 1, tx)),
            (y_via, (yh, tx)),
            (y_via, (yh - 1, tx)),
            (y_to, (N_TY - 1, tx)),
            (x_from, (ty, N_TX - 1)),
            (x_via, (ty, xh)),
            (x_via, (ty, xh - 1)),
            (x_to, (ty, N_TX - 1)),
        ]
    )

    def rc(k, src, dst, dev, rk=None):
        return pltpu.make_async_remote_copy(
            src_ref=src,
            dst_ref=dst,
            send_sem=ss.at[k],
            recv_sem=rs.at[k if rk is None else rk],
            device_id=dev,
            device_id_type=MESH,
        )

    ra = rc(0, tile.at[:, LOW, LEFT], strip_r.at[:, LOW, :], me.left)
    rb = rc(1, tile.at[:, HIGH, LEFT], strip_r.at[:, HIGH, :], me.left)
    rb_out = rc(1, tile.at[:, HIGH, LEFT], relay_r, (ty, N_TX - 1), 10)
    rb_fwd = rc(10, relay_r, strip_r.at[:, HIGH, :], (ty, xh - 1), 1)
    l0b = rc(2, tile.at[:, HIGH, LEFT], strip_l.at[:, HIGH, LEFT], me.up)
    l0a = rc(3, tile.at[:, LOW, LEFT], strip_l.at[:, LOW, LEFT], me.up)
    l1 = [
        rc(4, tile.at[:, LOW, RIGHT], strip_l.at[:, LOW, RIGHT], me.up),
        rc(5, tile.at[:, HIGH, RIGHT], strip_l.at[:, HIGH, RIGHT], me.up),
        l0a,
    ]
    l1_out = [
        rc(4, tile.at[:, LOW, RIGHT], relay_l.at[:, LOW, :], (N_TY - 1, tx), 8),
        rc(5, tile.at[:, HIGH, RIGHT], relay_l.at[:, HIGH, :], (N_TY - 1, tx), 9),
        rc(3, tile.at[:, LOW, LEFT], relay_a, (N_TY - 1, tx), 11),
    ]
    l1_fwd = [
        rc(8, relay_l.at[:, LOW, :], strip_l.at[:, LOW, RIGHT], (yh - 1, tx), 4),
        rc(9, relay_l.at[:, HIGH, :], strip_l.at[:, HIGH, RIGHT], (yh - 1, tx), 5),
        rc(11, relay_a, strip_l.at[:, LOW, LEFT], (yh - 1, tx), 3),
    ]
    ca = rc(6, strip_r.at[:, LOW, :], strip_c.at[:, LOW, :], me.up)
    cb = rc(7, strip_r.at[:, HIGH, :], strip_c.at[:, HIGH, :], me.up)
    cz = rc(7, strip_l.at[:, HIGH, LEFT], strip_c.at[:, HIGH, :], me.left)

    when(me.has_l, ra.start)
    when(me.has_u, l0b.start)
    when(me.has_l & (tx != xh), rb.start)
    when(x_from, rb_out.start)
    inner = tx < N_TX - 1
    for i, (direct, out) in enumerate(zip(l1, l1_out)):
        detour = y_from if i == 0 else y_from & inner
        when(me.has_u & jnp.logical_not(detour), direct.start)
        when(detour, out.start)

    load_p = pltpu.make_async_copy(pup, PP.at[:, 0:M], ls.at[0])
    load_a = pltpu.make_async_copy(amp, A, ls.at[1])
    load_x = pltpu.make_async_copy(tile, X.at[:, 0:M, 0 : 2 * M], ls.at[2])
    load_p.start()
    load_a.start()
    load_x.start()
    row0 = ty * M
    col0 = tx * 2 * M

    @pl.loop(0, 16)
    def _(i):
        G[:, pl.ds(pl.multiple_of(i * 64, 64), 64), :] = jnp.zeros((2, 64, 3 * M), F32)

    DP[...] = jnp.zeros((2, M, M), F32)
    load_p.wait()

    @pl.loop(0, 3)
    def _(s):
        r = off[s, 0] - row0
        c0 = lax.rem(off[s, 1], M)

        left = shifted(r, 0)
        right = shifted(c0, 1)
        for p in range(2):

            def put(part, value):
                PR[s, p, :, part] = value

            permute(lambda part: PP[p, part, :], H.at[0], put, left, right)

    load_a.wait()

    @pl.loop(0, 3)
    def _(s):
        def put(part, value):
            AP[s, :, part] = value

        permute(lambda part: A[s, part, :], H.at[0], put, pt[...], pm[...])

    when(me.has_r, ra.wait_recv)
    when(me.has_r & me.has_u, ca.start)
    when(me.has_d, l0b.wait_recv)
    when(me.has_d & me.has_l & me.odd, cz.start)

    def pass_rb():
        rb_out.wait_recv()
        rb_fwd.start()

    when(x_via, pass_rb)
    for i, (out, fwd) in enumerate(zip(l1_out, l1_fwd)):

        def pass_l1():
            out.wait_recv()
            fwd.start()

        when(y_via if i == 0 else y_via & inner, pass_l1)
    when(me.has_r, rb.wait_recv)
    when(me.has_r & me.has_u & me.odd, cb.start)

    def rest():
        l0a.wait_recv()
        l1[0].wait_recv()
        l1[1].wait_recv()

    when(me.has_d, rest)
    when(me.has_d & me.has_r, ca.wait_recv)
    when(me.has_d & me.has_r, cz.wait_recv)
    when(me.has_l, ra.wait_send)
    when(me.has_l, rb.wait_send)

    def sent_l():
        l0b.wait_send()
        l0a.wait_send()
        l1[0].wait_send()
        l1[1].wait_send()

    when(me.has_u, sent_l)
    when(me.has_r & me.has_u, ca.wait_send)
    when(me.has_r & me.has_u & me.odd, cb.wait_send)
    when(me.has_d & me.has_l & me.odd, cz.wait_send)
    when(x_via, rb_fwd.wait_send)

    for i, fwd in enumerate(l1_fwd):
        when(y_via if i == 0 else y_via & inner, fwd.wait_send)

    load_x.wait()
    CB, RB = 256, 512

    @pl.loop(0, 3)
    def _(s):
        r = off[s, 0] - row0
        c = off[s, 1] - col0
        qc = c // M
        c0 = c - qc * M
        weight = live[s].astype(F32)

        @pl.loop(0, M // CB)
        def _(j):
            cols = pl.ds(pl.multiple_of(j * CB, CB), CB)
            there = [pl.ds(pl.multiple_of(b * M + j * CB, CB), CB) for b in range(3)]
            mc = lax.broadcasted_iota(jnp.int32, (Q, CB), 1) + j * CB >= c0
            blk = jnp.where(mc, qc, qc + 1)
            first, second = blk == 0, blk == 1
            xr, xi = [], []
            for m in range(4):
                mr = lax.broadcasted_iota(jnp.int32, (Q, CB), 0) + m * Q >= r
                rt = slice(m * Q, (m + 1) * Q)
                rl = slice(M + m * Q, M + (m + 1) * Q)
                w = []
                for p in range(2):
                    high = [X[p, rt, t] for t in there]
                    low = [X[p, rl, t] for t in there]
                    v = jnp.where(
                        mr,
                        jnp.where(first, high[0], jnp.where(second, high[1], high[2])),
                        jnp.where(first, low[0], jnp.where(second, low[1], low[2])),
                    )
                    W[p, rt, cols] = v
                    w.append(v)
                pr = PR[s, 0, rt, cols]
                pi = PR[s, 1, rt, cols]
                xr.append(w[0] * pr - w[1] * pi)
                xi.append(w[0] * pi + w[1] * pr)
            for q, (yr, yi) in enumerate(fly_in(xr, xi)):
                o = lmul(mh[q], ml[q], jnp.concatenate([yr, yi], axis=0))
                H[0, q * Q : (q + 1) * Q, cols] = o[:Q]
                H[1, q * Q : (q + 1) * Q, cols] = o[Q:]

        for j in range(M // RB):
            rows = slice(j * RB, (j + 1) * RB)
            xr = [H[0, rows, m * Q : (m + 1) * Q] for m in range(4)]
            xi = [H[1, rows, m * Q : (m + 1) * Q] for m in range(4)]
            e = []
            for q, (yr, yi) in enumerate(fly_in(xr, xi)):
                f = rmul(jnp.concatenate([yr, yi], axis=1), th[q], tl[q])
                fr, fi = f[:, :Q], f[:, Q:]
                fac = 1.0 - AP[s, rows, q * Q : (q + 1) * Q] * lax.rsqrt(fr * fr + fi * fi + 1.0)
                o = rmul(jnp.concatenate([fac * fr, fac * fi], axis=1), mh[q], ml[q])
                e.append((o[:, :Q], o[:, Q:]))
            for m, (zr, zi) in enumerate(fly_out(e)):
                H[0, rows, m * Q : (m + 1) * Q] = zr
                H[1, rows, m * Q : (m + 1) * Q] = zi

        @pl.loop(0, M // CB)
        def _(j):
            cols = pl.ds(pl.multiple_of(j * CB, CB), CB)
            mc = lax.broadcasted_iota(jnp.int32, (Q, CB), 1) + j * CB >= c0
            blk = jnp.where(mc, qc, qc + 1)
            e = []
            for q in range(4):
                z = jnp.concatenate([H[0, q * Q : (q + 1) * Q, cols], H[1, q * Q : (q + 1) * Q, cols]], axis=0)
                o = lmul(th[q], tl[q], z)
                e.append((o[:Q], o[Q:]))
            for m, (sr, si) in enumerate(fly_out(e)):
                mr = lax.broadcasted_iota(jnp.int32, (Q, CB), 0) + m * Q >= r
                rt = slice(m * Q, (m + 1) * Q)
                rl = slice(M + m * Q, M + (m + 1) * Q)
                sr = sr * weight
                si = si * weight
                pr, pi = PR[s, 0, rt, cols], PR[s, 1, rt, cols]
                wr, wi = W[0, rt, cols], W[1, rt, cols]
                g = (pr * sr + pi * si, pr * si - pi * sr)
                d = (wr * sr + wi * si, wr * si - wi * sr)
                for p in range(2):
                    D[p, rt, cols] = d[p]
                    gt = jnp.where(mr, g[p], 0.0)
                    gl = g[p] - gt
                    for b in range(3):
                        there = pl.ds(pl.multiple_of(b * M + j * CB, CB), CB)
                        G[p, rt, there] += jnp.where(blk == b, gt, 0.0)
                        G[p, rl, there] += jnp.where(blk == b, gl, 0.0)

        left = shifted(r, 1)
        right = shifted(c0, 0)
        for p in range(2):

            def put(part, value):
                DP[p, :, part] += value

            permute(lambda part: D[p, part, :], H.at[0], put, left, right)

    out_g = pltpu.make_async_copy(G, grads, ls.at[0])
    out_d = pltpu.make_async_copy(DP, dpup, ls.at[1])
    out_g.start()
    out_d.start()
    out_g.wait()
    out_d.wait()


def slots(off, live, tile, amp, pup):
    hi, lo, th, tl, pm = [jnp.asarray(t) for t in tables()]
    smem = pl.BlockSpec(memory_space=pltpu.SMEM)
    hbm = pl.BlockSpec(memory_space=pl.ANY)
    vmem = pl.BlockSpec(memory_space=pltpu.VMEM)
    V = pltpu.VMEM
    return pl.pallas_call(
        slots_kernel,
        out_shape=[
            jax.ShapeDtypeStruct((2, 2 * M, 3 * M), F32),
            jax.ShapeDtypeStruct((2, M, M), F32),
        ],
        in_specs=[smem, smem, hbm, hbm, hbm] + [vmem] * 6,
        out_specs=[hbm, hbm],
        scratch_shapes=[
            V((2, 2 * M, 3 * M), F32),
            V((2, 2 * M, 3 * M), F32),
            V((3, M, M), F32),
            V((3, M, M), F32),
            V((2, M, M), F32),
            V((3, 2, M, M), F32),
            V((2, M, M), F32),
            V((2, M, M), F32),
            V((2, M, M), F32),
            V((2, M, M), F32),
            V((2, M, M), F32),
            V((2, M // 2, M), F32),
            V((2, M // 2, M), F32),
            pltpu.SemaphoreType.DMA((3,)),
            pltpu.SemaphoreType.DMA((12,)),
            pltpu.SemaphoreType.DMA((12,)),
        ],
        name="fetch_and_slots",
        compiler_params=pltpu.CompilerParams(
            collective_id=0, has_side_effects=True, vmem_limit_bytes=63 * 1024 * 1024
        ),
    )(off, live, tile, amp, pup, hi, lo, th, tl, pm, pm.T)


def give_kernel(
    grads, dpup, out, pup, own, g_r, g_l, got_l, got_r, got_c, got_z, relay_l, relay_r, part, sums, rows_a, rows_b, rows_c, ls, ss, rs, ps, pr
):
    me = Place()
    ty, tx = me.ty, me.tx
    yh, xh = N_TY // 2, N_TX // 2
    y_from, y_via, y_to = ty == yh - 1, ty == 0, ty == yh
    x_from, x_via, x_to = tx == xh - 1, tx == 0, tx == xh
    core = lax.rem(ty, 2)
    x = (ty // 8) * 2 + tx // 4
    y = lax.rem(ty, 8) // 2
    z = lax.rem(tx, 4)

    def device(px, py, pz):
        return ((px // 2) * 8 + py * 2 + core, lax.rem(px, 2) * 4 + pz)

    mate = (ty + 1 - 2 * core, tx)
    peers_x = [device(lax.rem(x + d, 4), y, z) for d in (1, 2, 3)]
    peers_y = [device(x, lax.rem(y + d, 4), z) for d in (1, 2, 3)]
    peers_z = [device(x, y, lax.rem(z + d, 4)) for d in (1, 2, 3)]
    always = ty >= 0
    greet(
        me.neighbours()
        + [
            (y_from, (0, tx)),
            (y_via, (yh - 1, tx)),
            (y_via, (yh, tx)),
            (y_to, (0, tx)),
            (x_from, (ty, 0)),
            (x_via, (ty, xh - 1)),
            (x_via, (ty, xh)),
            (x_to, (ty, 0)),
        ]
        + [(always, d) for d in [mate] + peers_x + peers_y + peers_z]
    )

    def rc(k, src, dst, dev, rk=None):
        return pltpu.make_async_remote_copy(
            src_ref=src,
            dst_ref=dst,
            send_sem=ss.at[k],
            recv_sem=rs.at[k if rk is None else rk],
            device_id=dev,
            device_id_type=MESH,
        )

    def pc(k, src, dst, dev):
        return pltpu.make_async_remote_copy(
            src_ref=src,
            dst_ref=dst,
            send_sem=ps.at[k],
            recv_sem=pr.at[k],
            device_id=dev,
            device_id_type=MESH,
        )

    top = pl.ds(M, 256)
    bottom = pl.ds(M + 256, 256)
    far = pl.ds(2 * M, M)
    load_p = pltpu.make_async_copy(dpup.at[core], part, ls.at[0])
    load_r = pltpu.make_async_copy(grads.at[:, WHOLE, far], g_r, ls.at[1])
    load_l = pltpu.make_async_copy(grads.at[:, bottom, LEFT], g_l, ls.at[2])
    load_o = pltpu.make_async_copy(grads.at[:, WHOLE, pl.ds(0, 2 * M)], own, ls.at[3])

    pair = pc(0, dpup.at[1 - core], sums, mate)
    ca = rc(0, grads.at[:, top, far], got_c.at[:, LOW, :], me.down)
    cb = rc(1, grads.at[:, bottom, far], got_c.at[:, HIGH, :], me.down)
    cz = rc(1, grads.at[:, bottom, far], got_z, me.right, 2)
    l0a = rc(3, grads.at[:, top, LEFT], got_l.at[:, LOW, LEFT], me.down)
    l0b = rc(4, g_l, got_l.at[:, HIGH, LEFT], me.down)
    l1 = [
        rc(5, grads.at[:, top, RIGHT], got_l.at[:, LOW, RIGHT], me.down),
        rc(6, grads.at[:, bottom, RIGHT], got_l.at[:, HIGH, RIGHT], me.down),
    ]
    l1_out = [
        rc(5, grads.at[:, top, RIGHT], relay_l.at[:, LOW, :], (0, tx), 9),
        rc(6, grads.at[:, bottom, RIGHT], relay_l.at[:, HIGH, :], (0, tx), 10),
    ]
    l1_fwd = [
        rc(9, relay_l.at[:, LOW, :], got_l.at[:, LOW, RIGHT], (yh, tx), 5),
        rc(10, relay_l.at[:, HIGH, :], got_l.at[:, HIGH, RIGHT], (yh, tx), 6),
    ]
    ra = rc(7, g_r.at[:, LOW, :], got_r.at[:, LOW, :], me.right)
    rb = rc(8, g_r.at[:, HIGH, :], got_r.at[:, HIGH, :], me.right)
    ra_out = rc(7, g_r.at[:, LOW, :], relay_r, (ty, 0), 11)
    ra_fwd = rc(11, relay_r, got_r.at[:, LOW, :], (ty, xh), 7)

    load_p.start()
    load_r.start()
    load_l.start()
    pair.start()
    has_c = me.has_d & me.has_r
    when(has_c, ca.start)
    when(has_c & me.even, cb.start)
    when(has_c & me.odd, cz.start)
    for direct, out_l in zip(l1, l1_out):
        when(me.has_d & (ty != yh - 1), direct.start)
        when(y_from, out_l.start)
    when(me.has_d, l0a.start)
    load_o.start()

    load_r.wait()
    load_l.wait()
    when(me.has_r & me.even, rb.start)
    when(me.has_d & (me.even | (tx == 0)), l0b.start)

    load_p.wait()
    pair.wait_recv()
    sums[...] += part[...]

    quarter = M // 4

    def share(base, step, peers, src, dst, rows, mine):
        copies = []
        for d in range(3):
            to = lax.rem(mine + d + 1, 4)
            copies.append(
                pc(base + d, src.at[pl.ds(pl.multiple_of(to * rows, rows), rows), :], dst.at[d], peers[d])
            )
        for copy in copies:
            copy.start()
        return copies

    def own_rows(src, rows, mine):
        return src[pl.ds(pl.multiple_of(mine * rows, rows), rows), :]

    sent = share(1, 0, peers_x, sums, rows_a, 128, x)

    def add_c_low():
        ca.wait_recv()
        g_r[:, LOW, :] += got_c[:, LOW, :]

    when(me.has_u & me.has_r, add_c_low)
    when(me.has_r & (tx != xh - 1), ra.start)
    when(x_from, ra_out.start)

    def add_c_high():
        cb.wait_recv()
        g_r[:, HIGH, :] += got_c[:, HIGH, :]
        rb.start()

    when(me.has_r & me.odd, add_c_high)

    def add_z():
        cz.wait_recv()
        g_l[...] += got_z[...]
        l0b.start()

    when(me.has_d & me.odd & (tx > 0), add_z)

    for copy in sent:
        copy.wait_recv()
    part[0:128, :] = own_rows(sums, 128, x) + rows_a[0] + rows_a[1] + rows_a[2]
    sent_y = share(4, 1, peers_y, part, rows_b, 32, y)

    def pass_ra():
        ra_out.wait_recv()
        ra_fwd.start()

    when(x_via, pass_ra)
    for out_l, fwd in zip(l1_out, l1_fwd):

        def pass_l1():
            out_l.wait_recv()
            fwd.start()

        when(y_via, pass_l1)

    for copy in sent_y:
        copy.wait_recv()
    part[128:160, :] = own_rows(part, 32, y) + rows_b[0] + rows_b[1] + rows_b[2]
    sent_z = share(7, 2, peers_z, part.at[pl.ds(128, 32)], rows_c, 8, z)
    for copy in sent_z:
        copy.wait_recv()
    norm = 1.0 / math.sqrt(N_TY * N_TX)
    base = x * 128 + y * 32 + z * 8
    total = own_rows(part.at[pl.ds(128, 32)], 8, z) + rows_c[0] + rows_c[1] + rows_c[2]
    pup[core, pl.ds(pl.multiple_of(base, 8), 8), :] = total * norm

    def spread(base_k, start, rows, peers):
        here = pup.at[core, pl.ds(pl.multiple_of(start, rows), rows), :]
        copies = [pc(base_k + d, here, here, peers[d]) for d in range(3)]
        for copy in copies:
            copy.start()
        for copy in copies:
            copy.wait_recv()
        return copies

    all_sent = sent + sent_y + sent_z
    all_sent += spread(10, base, 8, peers_z)
    all_sent += spread(13, x * 128 + y * 32, 32, peers_y)
    all_sent += spread(16, x * 128, 128, peers_x)
    last = pc(19, pup.at[core], pup.at[core], mate)
    last.start()

    load_o.wait()

    def add_l():
        l0a.wait_recv()
        l0b.wait_recv()
        l1[0].wait_recv()
        l1[1].wait_recv()

    when(me.has_u, add_l)

    def add_r():
        ra.wait_recv()
        rb.wait_recv()

    when(me.has_l, add_r)

    @pl.loop(0, 16)
    def _(i):
        rows = pl.ds(pl.multiple_of(i * 32, 32), 32)
        out[:, rows, :] = own[:, rows, :]

        @pl.when(me.has_u)
        def _():
            out[:, rows, :] += got_l[:, rows, :]

        @pl.when(me.has_l)
        def _():
            out[:, rows, 0:M] += got_r[:, rows, :]

    last.wait_recv()
    pair.wait_send()
    last.wait_send()
    for copy in all_sent:
        copy.wait_send()
    when(has_c, ca.wait_send)
    when(has_c, cb.wait_send)

    def sent_l():
        l0a.wait_send()
        l0b.wait_send()
        l1[0].wait_send()
        l1[1].wait_send()

    when(me.has_d, sent_l)

    def sent_r():
        ra.wait_send()
        rb.wait_send()

    when(me.has_r, sent_r)
    when(x_via, ra_fwd.wait_send)

    def sent_fwd():
        l1_fwd[0].wait_send()
        l1_fwd[1].wait_send()

    when(y_via, sent_fwd)


def give(grads, dpup):
    vmem = pltpu.VMEM
    return pl.pallas_call(
        give_kernel,
        out_shape=[
            jax.ShapeDtypeStruct((2, M, 2 * M), F32),
            jax.ShapeDtypeStruct((2, M, M), F32),
        ],
        in_specs=[pl.BlockSpec(memory_space=pl.ANY)] * 2,
        out_specs=[pl.BlockSpec(memory_space=pltpu.VMEM)] * 2,
        scratch_shapes=[
            vmem((2, M, 2 * M), F32),
            vmem((2, M, M), F32),
            vmem((2, M // 2, M), F32),
            vmem((2, M, 2 * M), F32),
            vmem((2, M, M), F32),
            vmem((2, M, M), F32),
            vmem((2, M // 2, M), F32),
            vmem((2, M, M), F32),
            vmem((2, M // 2, M), F32),
            vmem((M, M), F32),
            vmem((M, M), F32),
            vmem((3, 128, M), F32),
            vmem((3, 32, M), F32),
            vmem((3, 8, M), F32),
            pltpu.SemaphoreType.DMA((4,)),
            pltpu.SemaphoreType.DMA((12,)),
            pltpu.SemaphoreType.DMA((12,)),
            pltpu.SemaphoreType.DMA((20,)),
            pltpu.SemaphoreType.DMA((20,)),
        ],
        name="give_back",
        compiler_params=pltpu.CompilerParams(
            collective_id=1, has_side_effects=True, vmem_limit_bytes=60 * 1024 * 1024
        ),
    )(grads, dpup)


def body(spectrum, pupil, amplitudes, offsets, live):
    grads, dpup = slots(offsets, live, spectrum, amplitudes, pupil)
    return tuple(give(grads, dpup))


def solution(mesh):
    return jax.shard_map(
        body,
        mesh=mesh,
        in_specs=(
            P(None, "ty", "tx"),
            P(),
            P(("ty", "tx"), None, None),
            P(("ty", "tx"), None),
            P(("ty", "tx")),
        ),
        out_specs=(P(None, "ty", "tx"), P()),
        check_vma=False,
    )
```

```python
import math
import numpy as np
import ml_dtypes
import jax, jax.numpy as jnp, functools
from jax import lax
from jax.sharding import PartitionSpec as P
from jax.experimental import pallas as pl
from jax.experimental.pallas import tpu as pltpu
F32=jnp.float32; BF=jnp.bfloat16
N_TY = 16
N_TX = 8
M = 512
Q = 128

def tables():
    n=np.arange(Q)[None,:]; k=np.arange(Q)[:,None]
    hi=[];lo=[]
    for q in range(4):
        ang=2*np.pi*((n*(4*k+q))%M)/M
        c=np.cos(ang)/math.sqrt(M); s=np.sin(ang)/math.sqrt(M)
        m=np.block([[c,-s],[s,c]])
        h=m.astype(ml_dtypes.bfloat16); l=(m-h.astype(np.float64)).astype(ml_dtypes.bfloat16)
        hi.append(h); lo.append(l)
    hi=np.stack(hi); lo=np.stack(lo)
    perm=np.zeros((M,M),ml_dtypes.bfloat16)
    for q in range(4):
        for j in range(Q): perm[4*j+q,q*Q+j]=1
    T=lambda a: np.ascontiguousarray(np.swapaxes(a,1,2))
    return hi,lo,T(hi),T(lo),perm

def split(x):
    h=x.astype(BF)
    return h,(x-h.astype(F32)).astype(BF)

def dot(a,b):
    return jnp.dot(a,b,preferred_element_type=F32)

def lmul(mh,ml,y):
    h,l=split(y)
    return dot(jnp.concatenate([mh,ml,mh],axis=1),jnp.concatenate([h,h,l],axis=0))

def rmul(y,mh,ml):
    h,l=split(y)
    return dot(jnp.concatenate([h,l,h],axis=1),jnp.concatenate([mh,mh,ml],axis=0))

def fly_in(xr,xi):
    a=(xr[0]+xr[2],xi[0]+xi[2]); b=(xr[0]-xr[2],xi[0]-xi[2])
    c=(xr[1]+xr[3],xi[1]+xi[3]); d=(xr[1]-xr[3],xi[1]-xi[3])
    return [(a[0]+c[0],a[1]+c[1]),(b[0]-d[1],b[1]+d[0]),(a[0]-c[0],a[1]-c[1]),(b[0]+d[1],b[1]-d[0])]

def fly_out(e):
    a=(e[0][0]+e[2][0],e[0][1]+e[2][1]); b=(e[0][0]-e[2][0],e[0][1]-e[2][1])
    c=(e[1][0]+e[3][0],e[1][1]+e[3][1]); d=(e[1][0]-e[3][0],e[1][1]-e[3][1])
    return [(a[0]+c[0],a[1]+c[1]),(b[0]+d[1],b[1]-d[0]),(a[0]-c[0],a[1]-c[1]),(b[0]-d[1],b[1]+d[0])]


def permute(load, mid, store, left, right):
    for q in range(2):
        part = slice(q * 256, (q + 1) * 256)
        h, l = split(load(part))
        mid[part, :] = dot(jnp.concatenate([h, l], axis=1), jnp.concatenate([right, right], axis=0))
    for q in range(2):
        part = slice(q * 256, (q + 1) * 256)
        h, l = split(mid[:, part])
        store(part, dot(jnp.concatenate([left, left], axis=1), jnp.concatenate([h, l], axis=0)))


def shifted(by, axis):
    a = lax.broadcasted_iota(jnp.int32, (M, M), axis)
    b = lax.broadcasted_iota(jnp.int32, (M, M), 1 - axis) + by
    b = jnp.where(b >= M, b - M, b)
    return jnp.where(a == b, 1.0, 0.0).astype(BF)


MESH = pl.DeviceIdType.MESH
LOW = pl.ds(0, 256)
HIGH = pl.ds(256, 256)
LEFT = pl.ds(0, 512)
RIGHT = pl.ds(512, 512)
WHOLE = pl.ds(0, 512)


def when(cond, run):
    pl.when(cond)(run)


def greet(partners):
    barrier = pltpu.get_barrier_semaphore()
    count = jnp.int32(0)
    for cond, device in partners:
        count = count + jnp.where(cond, 1, 0).astype(jnp.int32)

        @pl.when(cond)
        def _():
            pl.semaphore_signal(barrier, inc=1, device_id=device, device_id_type=MESH)

    pl.semaphore_wait(barrier, count)


class Place:
    def __init__(self):
        ty = lax.axis_index("ty")
        tx = lax.axis_index("tx")
        self.ty, self.tx = ty, tx
        self.has_u, self.has_d = ty > 0, ty < N_TY - 1
        self.has_l, self.has_r = tx > 0, tx < N_TX - 1
        self.odd = lax.rem(ty, 2) == 1
        self.even = lax.rem(ty, 2) == 0
        self.up, self.down = (ty - 1, tx), (ty + 1, tx)
        self.left, self.right = (ty, tx - 1), (ty, tx + 1)

    def neighbours(self):
        return [
            (self.has_u, self.up),
            (self.has_d, self.down),
            (self.has_l, self.left),
            (self.has_r, self.right),
        ]


def slots_kernel(
    off, live, tile, amp, pup, mh, ml, th, tl, pm, pt, grads, dpup,
    X, G, A, AP, PP, PR, W, H, D, DP, relay_l, relay_a, relay_r, ls, ss, rs
):
    strip_r = X.at[:, 0:M, 2 * M : 3 * M]
    strip_l = X.at[:, M : 2 * M, 0 : 2 * M]
    strip_c = X.at[:, M : 2 * M, 2 * M : 3 * M]
    me = Place()
    ty, tx = me.ty, me.tx
    yh, xh = N_TY // 2, N_TX // 2
    y_from, y_via, y_to = ty == yh, ty == N_TY - 1, ty == yh - 1
    x_from, x_via, x_to = tx == xh, tx == N_TX - 1, tx == xh - 1
    greet(
        me.neighbours()
        + [
            (y_from, (N_TY - 1, tx)),
            (y_via, (yh, tx)),
            (y_via, (yh - 1, tx)),
            (y_to, (N_TY - 1, tx)),
            (x_from, (ty, N_TX - 1)),
            (x_via, (ty, xh)),
            (x_via, (ty, xh - 1)),
            (x_to, (ty, N_TX - 1)),
        ]
    )

    def rc(k, src, dst, dev, rk=None):
        return pltpu.make_async_remote_copy(
            src_ref=src,
            dst_ref=dst,
            send_sem=ss.at[k],
            recv_sem=rs.at[k if rk is None else rk],
            device_id=dev,
            device_id_type=MESH,
        )

    ra = rc(0, tile.at[:, LOW, LEFT], strip_r.at[:, LOW, :], me.left)
    rb = rc(1, tile.at[:, HIGH, LEFT], strip_r.at[:, HIGH, :], me.left)
    rb_out = rc(1, tile.at[:, HIGH, LEFT], relay_r, (ty, N_TX - 1), 10)
    rb_fwd = rc(10, relay_r, strip_r.at[:, HIGH, :], (ty, xh - 1), 1)
    l0b = rc(2, tile.at[:, HIGH, LEFT], strip_l.at[:, HIGH, LEFT], me.up)
    l0a = rc(3, tile.at[:, LOW, LEFT], strip_l.at[:, LOW, LEFT], me.up)
    l1 = [
        rc(4, tile.at[:, LOW, RIGHT], strip_l.at[:, LOW, RIGHT], me.up),
        rc(5, tile.at[:, HIGH, RIGHT], strip_l.at[:, HIGH, RIGHT], me.up),
        l0a,
    ]
    l1_out = [
        rc(4, tile.at[:, LOW, RIGHT], relay_l.at[:, LOW, :], (N_TY - 1, tx), 8),
        rc(5, tile.at[:, HIGH, RIGHT], relay_l.at[:, HIGH, :], (N_TY - 1, tx), 9),
        rc(3, tile.at[:, LOW, LEFT], relay_a, (N_TY - 1, tx), 11),
    ]
    l1_fwd = [
        rc(8, relay_l.at[:, LOW, :], strip_l.at[:, LOW, RIGHT], (yh - 1, tx), 4),
        rc(9, relay_l.at[:, HIGH, :], strip_l.at[:, HIGH, RIGHT], (yh - 1, tx), 5),
        rc(11, relay_a, strip_l.at[:, LOW, LEFT], (yh - 1, tx), 3),
    ]
    ca = rc(6, strip_r.at[:, LOW, :], strip_c.at[:, LOW, :], me.up)
    cb = rc(7, strip_r.at[:, HIGH, :], strip_c.at[:, HIGH, :], me.up)
    cz = rc(7, strip_l.at[:, HIGH, LEFT], strip_c.at[:, HIGH, :], me.left)

    when(me.has_l, ra.start)
    when(me.has_u, l0b.start)
    when(me.has_l & (tx != xh), rb.start)
    when(x_from, rb_out.start)
    inner = tx < N_TX - 1
    for i, (direct, out) in enumerate(zip(l1, l1_out)):
        detour = y_from if i == 0 else y_from & inner
        when(me.has_u & jnp.logical_not(detour), direct.start)
        when(detour, out.start)

    load_p = pltpu.make_async_copy(pup, PP.at[:, 0:M], ls.at[0])
    load_a = pltpu.make_async_copy(amp, A, ls.at[1])
    load_x = pltpu.make_async_copy(tile, X.at[:, 0:M, 0 : 2 * M], ls.at[2])
    load_p.start()
    load_a.start()
    load_x.start()
    row0 = ty * M
    col0 = tx * 2 * M

    @pl.loop(0, 16)
    def _(i):
        G[:, pl.ds(pl.multiple_of(i * 64, 64), 64), :] = jnp.zeros((2, 64, 3 * M), F32)

    DP[...] = jnp.zeros((2, M, M), F32)
    load_p.wait()

    @pl.loop(0, 3)
    def _(s):
        r = off[s, 0] - row0
        c0 = lax.rem(off[s, 1], M)

        left = shifted(r, 0)
        right = shifted(c0, 1)
        for p in range(2):

            def put(part, value):
                PR[s, p, :, part] = value

            permute(lambda part: PP[p, part, :], H.at[0], put, left, right)

    load_a.wait()

    @pl.loop(0, 3)
    def _(s):
        def put(part, value):
            AP[s, :, part] = value

        permute(lambda part: A[s, part, :], H.at[0], put, pt[...], pm[...])

    when(me.has_r, ra.wait_recv)
    when(me.has_r & me.has_u, ca.start)
    when(me.has_d, l0b.wait_recv)
    when(me.has_d & me.has_l & me.odd, cz.start)

    def pass_rb():
        rb_out.wait_recv()
        rb_fwd.start()

    when(x_via, pass_rb)
    for i, (out, fwd) in enumerate(zip(l1_out, l1_fwd)):

        def pass_l1():
            out.wait_recv()
            fwd.start()

        when(y_via if i == 0 else y_via & inner, pass_l1)
    when(me.has_r, rb.wait_recv)
    when(me.has_r & me.has_u & me.odd, cb.start)

    def rest():
        l0a.wait_recv()
        l1[0].wait_recv()
        l1[1].wait_recv()

    when(me.has_d, rest)
    when(me.has_d & me.has_r, ca.wait_recv)
    when(me.has_d & me.has_r, cz.wait_recv)
    when(me.has_l, ra.wait_send)
    when(me.has_l, rb.wait_send)

    def sent_l():
        l0b.wait_send()
        l0a.wait_send()
        l1[0].wait_send()
        l1[1].wait_send()

    when(me.has_u, sent_l)
    when(me.has_r & me.has_u, ca.wait_send)
    when(me.has_r & me.has_u & me.odd, cb.wait_send)
    when(me.has_d & me.has_l & me.odd, cz.wait_send)
    when(x_via, rb_fwd.wait_send)

    for i, fwd in enumerate(l1_fwd):
        when(y_via if i == 0 else y_via & inner, fwd.wait_send)

    load_x.wait()
    CB, RB = 256, 512

    @pl.loop(0, 3)
    def _(s):
        r = off[s, 0] - row0
        c = off[s, 1] - col0
        qc = c // M
        c0 = c - qc * M
        weight = live[s].astype(F32)

        @pl.loop(0, M // CB)
        def _(j):
            cols = pl.ds(pl.multiple_of(j * CB, CB), CB)
            there = [pl.ds(pl.multiple_of(b * M + j * CB, CB), CB) for b in range(3)]
            mc = lax.broadcasted_iota(jnp.int32, (Q, CB), 1) + j * CB >= c0
            blk = jnp.where(mc, qc, qc + 1)
            first, second = blk == 0, blk == 1
            xr, xi = [], []
            for m in range(4):
                mr = lax.broadcasted_iota(jnp.int32, (Q, CB), 0) + m * Q >= r
                rt = slice(m * Q, (m + 1) * Q)
                rl = slice(M + m * Q, M + (m + 1) * Q)
                w = []
                for p in range(2):
                    high = [X[p, rt, t] for t in there]
                    low = [X[p, rl, t] for t in there]
                    v = jnp.where(
                        mr,
                        jnp.where(first, high[0], jnp.where(second, high[1], high[2])),
                        jnp.where(first, low[0], jnp.where(second, low[1], low[2])),
                    )
                    W[p, rt, cols] = v
                    w.append(v)
                pr = PR[s, 0, rt, cols]
                pi = PR[s, 1, rt, cols]
                xr.append(w[0] * pr - w[1] * pi)
                xi.append(w[0] * pi + w[1] * pr)
            for q, (yr, yi) in enumerate(fly_in(xr, xi)):
                o = lmul(mh[q], ml[q], jnp.concatenate([yr, yi], axis=0))
                H[0, q * Q : (q + 1) * Q, cols] = o[:Q]
                H[1, q * Q : (q + 1) * Q, cols] = o[Q:]

        for j in range(M // RB):
            rows = slice(j * RB, (j + 1) * RB)
            xr = [H[0, rows, m * Q : (m + 1) * Q] for m in range(4)]
            xi = [H[1, rows, m * Q : (m + 1) * Q] for m in range(4)]
            e = []
            for q, (yr, yi) in enumerate(fly_in(xr, xi)):
                f = rmul(jnp.concatenate([yr, yi], axis=1), th[q], tl[q])
                fr, fi = f[:, :Q], f[:, Q:]
                fac = 1.0 - AP[s, rows, q * Q : (q + 1) * Q] * lax.rsqrt(fr * fr + fi * fi + 1.0)
                o = rmul(jnp.concatenate([fac * fr, fac * fi], axis=1), mh[q], ml[q])
                e.append((o[:, :Q], o[:, Q:]))
            for m, (zr, zi) in enumerate(fly_out(e)):
                H[0, rows, m * Q : (m + 1) * Q] = zr
                H[1, rows, m * Q : (m + 1) * Q] = zi

        @pl.loop(0, M // CB)
        def _(j):
            cols = pl.ds(pl.multiple_of(j * CB, CB), CB)
            mc = lax.broadcasted_iota(jnp.int32, (Q, CB), 1) + j * CB >= c0
            blk = jnp.where(mc, qc, qc + 1)
            e = []
            for q in range(4):
                z = jnp.concatenate([H[0, q * Q : (q + 1) * Q, cols], H[1, q * Q : (q + 1) * Q, cols]], axis=0)
                o = lmul(th[q], tl[q], z)
                e.append((o[:Q], o[Q:]))
            for m, (sr, si) in enumerate(fly_out(e)):
                mr = lax.broadcasted_iota(jnp.int32, (Q, CB), 0) + m * Q >= r
                rt = slice(m * Q, (m + 1) * Q)
                rl = slice(M + m * Q, M + (m + 1) * Q)
                sr = sr * weight
                si = si * weight
                pr, pi = PR[s, 0, rt, cols], PR[s, 1, rt, cols]
                wr, wi = W[0, rt, cols], W[1, rt, cols]
                g = (pr * sr + pi * si, pr * si - pi * sr)
                d = (wr * sr + wi * si, wr * si - wi * sr)
                for p in range(2):
                    D[p, rt, cols] = d[p]
                    gt = jnp.where(mr, g[p], 0.0)
                    gl = g[p] - gt
                    for b in range(3):
                        there = pl.ds(pl.multiple_of(b * M + j * CB, CB), CB)
                        G[p, rt, there] += jnp.where(blk == b, gt, 0.0)
                        G[p, rl, there] += jnp.where(blk == b, gl, 0.0)

        left = shifted(r, 1)
        right = shifted(c0, 0)
        for p in range(2):

            def put(part, value):
                DP[p, :, part] += value

            permute(lambda part: D[p, part, :], H.at[0], put, left, right)

    out_g = pltpu.make_async_copy(G, grads, ls.at[0])
    out_d = pltpu.make_async_copy(DP, dpup, ls.at[1])
    out_g.start()
    out_d.start()
    out_g.wait()
    out_d.wait()


def slots(off, live, tile, amp, pup):
    hi, lo, th, tl, pm = [jnp.asarray(t) for t in tables()]
    smem = pl.BlockSpec(memory_space=pltpu.SMEM)
    hbm = pl.BlockSpec(memory_space=pl.ANY)
    vmem = pl.BlockSpec(memory_space=pltpu.VMEM)
    V = pltpu.VMEM
    return pl.pallas_call(
        slots_kernel,
        out_shape=[
            jax.ShapeDtypeStruct((2, 2 * M, 3 * M), F32),
            jax.ShapeDtypeStruct((2, M, M), F32),
        ],
        in_specs=[smem, smem, hbm, hbm, hbm] + [vmem] * 6,
        out_specs=[hbm, hbm],
        scratch_shapes=[
            V((2, 2 * M, 3 * M), F32),
            V((2, 2 * M, 3 * M), F32),
            V((3, M, M), F32),
            V((3, M, M), F32),
            V((2, M, M), F32),
            V((3, 2, M, M), F32),
            V((2, M, M), F32),
            V((2, M, M), F32),
            V((2, M, M), F32),
            V((2, M, M), F32),
            V((2, M, M), F32),
            V((2, M // 2, M), F32),
            V((2, M // 2, M), F32),
            pltpu.SemaphoreType.DMA((3,)),
            pltpu.SemaphoreType.DMA((12,)),
            pltpu.SemaphoreType.DMA((12,)),
        ],
        name="fetch_and_slots",
        compiler_params=pltpu.CompilerParams(
            collective_id=0, has_side_effects=True, vmem_limit_bytes=63 * 1024 * 1024
        ),
    )(off, live, tile, amp, pup, hi, lo, th, tl, pm, pm.T)


def give_kernel(
    grads, dpup, out, pup, own, g_r, g_l, got_l, got_r, got_c, got_z, relay_l, relay_r, part, sums, rows_a, rows_b, rows_c, ls, ss, rs, ps, pr
):
    me = Place()
    ty, tx = me.ty, me.tx
    yh, xh = N_TY // 2, N_TX // 2
    y_from, y_via, y_to = ty == yh - 1, ty == 0, ty == yh
    x_from, x_via, x_to = tx == xh - 1, tx == 0, tx == xh
    core = lax.rem(ty, 2)
    x = (ty // 8) * 2 + tx // 4
    y = lax.rem(ty, 8) // 2
    z = lax.rem(tx, 4)

    def device(px, py, pz):
        return ((px // 2) * 8 + py * 2 + core, lax.rem(px, 2) * 4 + pz)

    mate = (ty + 1 - 2 * core, tx)
    peers_x = [device(lax.rem(x + d, 4), y, z) for d in (1, 2, 3)]
    peers_y = [device(x, lax.rem(y + d, 4), z) for d in (1, 2, 3)]
    peers_z = [device(x, y, lax.rem(z + d, 4)) for d in (1, 2, 3)]
    always = ty >= 0
    greet(
        me.neighbours()
        + [
            (y_from, (0, tx)),
            (y_via, (yh - 1, tx)),
            (y_via, (yh, tx)),
            (y_to, (0, tx)),
            (x_from, (ty, 0)),
            (x_via, (ty, xh - 1)),
            (x_via, (ty, xh)),
            (x_to, (ty, 0)),
        ]
        + [(always, d) for d in [mate] + peers_x + peers_y + peers_z]
    )

    def rc(k, src, dst, dev, rk=None):
        return pltpu.make_async_remote_copy(
            src_ref=src,
            dst_ref=dst,
            send_sem=ss.at[k],
            recv_sem=rs.at[k if rk is None else rk],
            device_id=dev,
            device_id_type=MESH,
        )

    def pc(k, src, dst, dev):
        return pltpu.make_async_remote_copy(
            src_ref=src,
            dst_ref=dst,
            send_sem=ps.at[k],
            recv_sem=pr.at[k],
            device_id=dev,
            device_id_type=MESH,
        )

    top = pl.ds(M, 256)
    bottom = pl.ds(M + 256, 256)
    far = pl.ds(2 * M, M)
    load_p = pltpu.make_async_copy(dpup.at[core], part, ls.at[0])
    load_r = pltpu.make_async_copy(grads.at[:, WHOLE, far], g_r, ls.at[1])
    load_l = pltpu.make_async_copy(grads.at[:, bottom, LEFT], g_l, ls.at[2])
    load_o = pltpu.make_async_copy(grads.at[:, WHOLE, pl.ds(0, 2 * M)], own, ls.at[3])

    pair = pc(0, dpup.at[1 - core], sums, mate)
    ca = rc(0, grads.at[:, top, far], got_c.at[:, LOW, :], me.down)
    cb = rc(1, grads.at[:, bottom, far], got_c.at[:, HIGH, :], me.down)
    cz = rc(1, grads.at[:, bottom, far], got_z, me.right, 2)
    l0a = rc(3, grads.at[:, top, LEFT], got_l.at[:, LOW, LEFT], me.down)
    l0b = rc(4, g_l, got_l.at[:, HIGH, LEFT], me.down)
    l1 = [
        rc(5, grads.at[:, top, RIGHT], got_l.at[:, LOW, RIGHT], me.down),
        rc(6, grads.at[:, bottom, RIGHT], got_l.at[:, HIGH, RIGHT], me.down),
    ]
    l1_out = [
        rc(5, grads.at[:, top, RIGHT], relay_l.at[:, LOW, :], (0, tx), 9),
        rc(6, grads.at[:, bottom, RIGHT], relay_l.at[:, HIGH, :], (0, tx), 10),
    ]
    l1_fwd = [
        rc(9, relay_l.at[:, LOW, :], got_l.at[:, LOW, RIGHT], (yh, tx), 5),
        rc(10, relay_l.at[:, HIGH, :], got_l.at[:, HIGH, RIGHT], (yh, tx), 6),
    ]
    ra = rc(7, g_r.at[:, LOW, :], got_r.at[:, LOW, :], me.right)
    rb = rc(8, g_r.at[:, HIGH, :], got_r.at[:, HIGH, :], me.right)
    rb_out = rc(8, g_r.at[:, HIGH, :], relay_r, (ty, 0), 11)
    rb_fwd = rc(11, relay_r, got_r.at[:, HIGH, :], (ty, xh), 8)

    load_p.start()
    load_r.start()
    load_l.start()
    pair.start()
    has_c = me.has_d & me.has_r
    when(has_c, ca.start)
    when(has_c & me.even, cb.start)
    when(has_c & me.odd, cz.start)
    for direct, out_l in zip(l1, l1_out):
        when(me.has_d & (ty != yh - 1), direct.start)
        when(y_from, out_l.start)
    when(me.has_d, l0a.start)
    load_o.start()

    load_r.wait()
    load_l.wait()
    when(me.has_r & me.even & (tx != xh - 1), rb.start)
    when(x_from & me.even, rb_out.start)
    when(me.has_d & (me.even | (tx == 0)), l0b.start)

    load_p.wait()
    pair.wait_recv()
    sums[...] += part[...]

    quarter = M // 4

    def share(base, step, peers, src, dst, rows, mine):
        copies = []
        for d in range(3):
            to = lax.rem(mine + d + 1, 4)
            copies.append(
                pc(base + d, src.at[pl.ds(pl.multiple_of(to * rows, rows), rows), :], dst.at[d], peers[d])
            )
        for copy in copies:
            copy.start()
        return copies

    def own_rows(src, rows, mine):
        return src[pl.ds(pl.multiple_of(mine * rows, rows), rows), :]

    sent = share(1, 0, peers_x, sums, rows_a, 128, x)

    def add_c_low():
        ca.wait_recv()
        g_r[:, LOW, :] += got_c[:, LOW, :]

    when(me.has_u & me.has_r, add_c_low)
    when(me.has_r, ra.start)

    def add_c_high():
        cb.wait_recv()
        g_r[:, HIGH, :] += got_c[:, HIGH, :]
        when(tx != xh - 1, rb.start)
        when(x_from, rb_out.start)

    when(me.has_r & me.odd, add_c_high)

    def add_z():
        cz.wait_recv()
        g_l[...] += got_z[...]
        l0b.start()

    when(me.has_d & me.odd & (tx > 0), add_z)

    for copy in sent:
        copy.wait_recv()
    part[0:128, :] = own_rows(sums, 128, x) + rows_a[0] + rows_a[1] + rows_a[2]
    sent_y = share(4, 1, peers_y, part, rows_b, 32, y)

    def pass_rb():
        rb_out.wait_recv()
        rb_fwd.start()

    when(x_via, pass_rb)
    for out_l, fwd in zip(l1_out, l1_fwd):

        def pass_l1():
            out_l.wait_recv()
            fwd.start()

        when(y_via, pass_l1)

    for copy in sent_y:
        copy.wait_recv()
    part[128:160, :] = own_rows(part, 32, y) + rows_b[0] + rows_b[1] + rows_b[2]
    sent_z = share(7, 2, peers_z, part.at[pl.ds(128, 32)], rows_c, 8, z)
    for copy in sent_z:
        copy.wait_recv()
    norm = 1.0 / math.sqrt(N_TY * N_TX)
    base = x * 128 + y * 32 + z * 8
    total = own_rows(part.at[pl.ds(128, 32)], 8, z) + rows_c[0] + rows_c[1] + rows_c[2]
    pup[core, pl.ds(pl.multiple_of(base, 8), 8), :] = total * norm

    def spread(base_k, start, rows, peers):
        here = pup.at[core, pl.ds(pl.multiple_of(start, rows), rows), :]
        copies = [pc(base_k + d, here, here, peers[d]) for d in range(3)]
        for copy in copies:
            copy.start()
        for copy in copies:
            copy.wait_recv()
        return copies

    all_sent = sent + sent_y + sent_z
    all_sent += spread(10, base, 8, peers_z)
    all_sent += spread(13, x * 128 + y * 32, 32, peers_y)
    all_sent += spread(16, x * 128, 128, peers_x)
    last = pc(19, pup.at[core], pup.at[core], mate)
    last.start()

    load_o.wait()

    def add_l():
        l0a.wait_recv()
        l0b.wait_recv()
        l1[0].wait_recv()
        l1[1].wait_recv()

    when(me.has_u, add_l)

    def add_r():
        ra.wait_recv()
        rb.wait_recv()

    when(me.has_l, add_r)

    @pl.loop(0, 16)
    def _(i):
        rows = pl.ds(pl.multiple_of(i * 32, 32), 32)
        out[:, rows, :] = own[:, rows, :]

        @pl.when(me.has_u)
        def _():
            out[:, rows, :] += got_l[:, rows, :]

        @pl.when(me.has_l)
        def _():
            out[:, rows, 0:M] += got_r[:, rows, :]

    last.wait_recv()
    pair.wait_send()
    last.wait_send()
    for copy in all_sent:
        copy.wait_send()
    when(has_c, ca.wait_send)
    when(has_c, cb.wait_send)

    def sent_l():
        l0a.wait_send()
        l0b.wait_send()
        l1[0].wait_send()
        l1[1].wait_send()

    when(me.has_d, sent_l)

    def sent_r():
        ra.wait_send()
        rb.wait_send()

    when(me.has_r, sent_r)
    when(x_via, rb_fwd.wait_send)

    def sent_fwd():
        l1_fwd[0].wait_send()
        l1_fwd[1].wait_send()

    when(y_via, sent_fwd)


def give(grads, dpup):
    vmem = pltpu.VMEM
    return pl.pallas_call(
        give_kernel,
        out_shape=[
            jax.ShapeDtypeStruct((2, M, 2 * M), F32),
            jax.ShapeDtypeStruct((2, M, M), F32),
        ],
        in_specs=[pl.BlockSpec(memory_space=pl.ANY)] * 2,
        out_specs=[pl.BlockSpec(memory_space=pltpu.VMEM)] * 2,
        scratch_shapes=[
            vmem((2, M, 2 * M), F32),
            vmem((2, M, M), F32),
            vmem((2, M // 2, M), F32),
            vmem((2, M, 2 * M), F32),
            vmem((2, M, M), F32),
            vmem((2, M, M), F32),
            vmem((2, M // 2, M), F32),
            vmem((2, M, M), F32),
            vmem((2, M // 2, M), F32),
            vmem((M, M), F32),
            vmem((M, M), F32),
            vmem((3, 128, M), F32),
            vmem((3, 32, M), F32),
            vmem((3, 8, M), F32),
            pltpu.SemaphoreType.DMA((4,)),
            pltpu.SemaphoreType.DMA((12,)),
            pltpu.SemaphoreType.DMA((12,)),
            pltpu.SemaphoreType.DMA((20,)),
            pltpu.SemaphoreType.DMA((20,)),
        ],
        name="give_back",
        compiler_params=pltpu.CompilerParams(
            collective_id=1, has_side_effects=True, vmem_limit_bytes=60 * 1024 * 1024
        ),
    )(grads, dpup)


def body(spectrum, pupil, amplitudes, offsets, live):
    grads, dpup = slots(offsets, live, spectrum, amplitudes, pupil)
    return tuple(give(grads, dpup))


def solution(mesh):
    return jax.shard_map(
        body,
        mesh=mesh,
        in_specs=(
            P(None, "ty", "tx"),
            P(),
            P(("ty", "tx"), None, None),
            P(("ty", "tx"), None),
            P(("ty", "tx")),
        ),
        out_specs=(P(None, "ty", "tx"), P()),
        check_vma=False,
    )
```
